256 devices in a mesh: seq: 32 (over x, y, core), head: 8 (over z).
Axes of the slice: x: 4, y: 4, z: 8, core: 2. Of those that a mesh axis runs over, the one named last changes fastest.
Arguments:
- queries: bfloat16 [262144, 1024], P('seq', 'head'), may hold values from -6 to 6
- keys: bfloat16 [262144, 1024], P('seq', 'head'), may hold values from -0.52734375 to 0.52734375
- values: bfloat16 [262144, 1024], P('seq', 'head'), may hold values from -6 to 6
- exponents: int32 [8], P('head'), may hold values from 16 to 4194304, as said below
- gain: float32 [1024], P('head'), may hold values from 0.1 to 1.9
Outputs:
- attended: bfloat16 [262144, 1024], P('seq', 'head')
- final_state: float32 [8, 128, 128], P(None, 'seq')
The draws below stay inside these ranges and needn't reach their ends.
Inputs may be any that keep to these rules, and one draw needn't show every extreme that they name: `exponents`: each exponent is a power of two; some head has 16 and some head has 4194304.
All inputs are finite; a program needn't handle non-finite values.
Results may differ from the reference program's by a relative error of at most 0.0044.
Values sent between devices are 32-bit elements; how exact they have to be, the bound alone decides.
A program may use at most 64 MiB of HBM per device.

```python
import jax
import jax.numpy as jnp
from jax import lax

HD = 128
HEADS = 8
BLOCK = 256
TOKENS = 262144


def draw_exponents(key, part):
    key = jax.random.fold_in(key, 7)
    first, second = jax.random.split(key)
    powers = jax.random.randint(first, (HEADS,), 4, 23)
    order = jax.random.permutation(second, HEADS)
    powers = jnp.where(order == 0, 22, jnp.where(order == 1, 4, powers))
    return jnp.left_shift(jnp.ones((HEADS,), jnp.int32), powers.astype(jnp.int32))


def levels(stream_key, shape, pieces, low, high):
    level, own = 1.0, jax.random.fold_in(stream_key, 6)
    for dim, shards_of in pieces:
        steps = jnp.exp(jax.random.uniform(jax.random.fold_in(own, dim), (shards_of,), jnp.float32, low / len(pieces), high / len(pieces)))
        level = level * jnp.repeat(steps, shape[dim] // shards_of).reshape([-1 if axis == dim else 1 for axis in range(len(shape))])
    return level


def scatter_about(own_key, dims, scale, reach, pieces=(), kind=jnp.bfloat16):
    array = scale * jax.random.normal(own_key, dims, jnp.float32)
    if pieces:
        array = array * levels(own_key, dims, pieces, -0.22, 0.18)
    return jnp.clip(array, -reach, reach).astype(kind)


def setup_inputs(seed: int = 0) -> dict:
    splits = jax.random.split(jax.random.key(seed), 6)
    queries = scatter_about(splits[0], (TOKENS, HEADS * HD), 1.0, 6.0, ((0, 32), (1, 8)))
    keys = scatter_about(splits[1], (TOKENS, HEADS * HD), 0.088, 0.52734375, ((0, 32), (1, 8)))
    values = scatter_about(splits[2], (TOKENS, HEADS * HD), 1.0, 6.0, ((0, 32), (1, 8)))
    exponents = draw_exponents(jax.random.fold_in(splits[5], 71), 0)
    gain = jnp.clip(1.0 + 0.18 * jax.random.normal(splits[4], (HEADS * HD,), jnp.float32), 0.1, 1.9)
    return {"queries": queries, "keys": keys, "values": values, "exponents": exponents, "gain": gain}


def reference(queries, keys, values, exponents, gain):
    blocks = TOKENS // BLOCK
    rate = exponents.astype(jnp.float32) / 16777216.0
    qq = queries.reshape(blocks, BLOCK, HEADS, HD)
    kk = keys.reshape(blocks, BLOCK, HEADS, HD)
    vv = values.reshape(blocks, BLOCK, HEADS, HD)
    pos = jnp.arange(BLOCK).astype(jnp.float32)
    lower = pos[:, None] >= pos[None, :]
    gap = jnp.maximum(pos[:, None] - pos[None, :], 0.0)
    within = jnp.where(lower[None], jnp.exp2(-rate[:, None, None] * gap[None]), 0.0)
    lead = jnp.exp2(-rate[None, :] * (pos[:, None] + 1.0))
    tail = jnp.exp2(-rate[None, :] * (BLOCK - 1.0 - pos[:, None]))
    whole = jnp.exp2(-rate * BLOCK)

    def step(state, blk):
        q, k, v = blk
        qf = q.astype(jnp.float32)
        scores = jnp.einsum('ihd,jhd->hij', qf, k.astype(jnp.float32))
        weights = (scores * within).astype(jnp.bfloat16)
        local = jnp.einsum('hij,jhe->ihe', weights.astype(jnp.float32), v.astype(jnp.float32))
        inter = jnp.einsum('ihd,hde->ihe', qf * lead[:, :, None], state, precision=lax.Precision.HIGHEST)
        scaled = (k.astype(jnp.float32) * tail[:, :, None]).astype(jnp.bfloat16)
        contrib = jnp.einsum('jhd,jhe->hde', scaled.astype(jnp.float32), v.astype(jnp.float32))
        return (whole[:, None, None] * state + contrib, local + inter)
    start = jnp.zeros((HEADS, HD, HD), jnp.float32)
    final_state, raw = lax.scan(step, start, (qq, kk, vv))
    mean_sq = lax.optimization_barrier(jnp.mean(raw * raw, axis=-1, keepdims=True))
    normed = raw * lax.rsqrt(mean_sq + 1e-06) * gain.reshape(HEADS, HD)
    return (normed.astype(jnp.bfloat16).reshape(TOKENS, HEADS * HD), final_state)
```

```python
import functools

import jax
import jax.numpy as jnp
from jax import lax
from jax.experimental import pallas as pl
from jax.experimental.pallas import tpu as pltpu
from jax.sharding import PartitionSpec as P

BLOCK = 256
PIECES = 8
FIRST = 12
MESH = pl.DeviceIdType.MESH
F32 = jnp.float32
BF16 = jnp.bfloat16


def rows(start, count):
    return pl.ds(pl.multiple_of(start, count), count)


def split(value):
    high = value.astype(BF16)
    return high, (value - high.astype(F32)).astype(BF16)


def state_kernel(
    n_seq, n_head,
    exps_hbm, gain_hbm, q_hbm, k_hbm, v_hbm,
    raw, q, prior, final, lead, gain, decay,
    k, v, exps, within, tail, before, own, gathered, prefix, landed, finals,
    in_sems, small_sems, send_sems, recv_sems,
):
    me, mine = lax.axis_index("seq"), lax.axis_index("head")
    tokens, width = q.shape
    blocks = tokens // BLOCK
    per_piece = blocks // PIECES
    piece_rows = per_piece * BLOCK

    def load(which, piece):
        src, dst = ((k_hbm, k), (v_hbm, v), (q_hbm, q))[which]
        part = rows(piece * piece_rows, piece_rows)
        return pltpu.make_async_copy(src.at[part], dst.at[part], in_sems.at[which, piece])

    read_exps = pltpu.make_async_copy(exps_hbm, exps, small_sems.at[0])
    read_gain = pltpu.make_async_copy(gain_hbm, gain, small_sems.at[1])
    read_exps.start()
    for piece in range(PIECES):
        load(0, piece).start()
        load(1, piece).start()
    for piece in range(PIECES):
        load(2, piece).start()
    read_gain.start()

    barrier = pltpu.get_barrier_semaphore()

    @pl.loop(1, n_seq)
    def _(step):
        pl.semaphore_signal(
            barrier, inc=1, device_id={"seq": lax.rem(me + step, n_seq)}, device_id_type=MESH
        )

    @pl.loop(1, n_head)
    def _(step):
        pl.semaphore_signal(
            barrier, inc=1, device_id={"head": lax.rem(mine + step, n_head)}, device_id_type=MESH
        )

    read_exps.wait()
    rate = exps[0].astype(F32) / 16777216.0
    row = lax.broadcasted_iota(jnp.int32, (BLOCK, width), 0).astype(F32)
    lead[...] = jnp.exp2(-rate * (row + 1.0))
    tail[...] = jnp.exp2(-rate * (BLOCK - 1.0 - row))
    gap = (
        lax.broadcasted_iota(jnp.int32, (BLOCK, BLOCK), 0)
        - lax.broadcasted_iota(jnp.int32, (BLOCK, BLOCK), 1)
    ).astype(F32)
    within[...] = jnp.where(gap >= 0.0, jnp.exp2(-rate * jnp.maximum(gap, 0.0)), 0.0)
    ones = jnp.ones((1, width), F32)
    decay[...] = jnp.exp2(-rate * BLOCK * ones)
    whole = jnp.exp2(-rate * tokens * ones)

    def contribute(piece, state):
        load(0, piece).wait()
        load(1, piece).wait()
        for j in range(per_piece):
            block = piece * per_piece + j
            part = rows(block * BLOCK, BLOCK)
            scaled = (k[part, :].astype(F32) * tail[...]).astype(BF16)
            term = lax.dot_general(
                scaled, v[part, :], (((0,), (0,)), ((), ())), preferred_element_type=F32
            )
            before[block] = state
            state = state * decay[...] + term
        return state

    total = lax.fori_loop(0, PIECES, contribute, jnp.zeros((width, width), F32))
    own[...] = total.reshape(own.shape)
    gathered[me] = own[me]
    pl.semaphore_wait(barrier, n_seq + n_head - 2)

    def exchange(src, dst, which, step):
        to = lax.rem(me + step, n_seq)
        return pltpu.make_async_remote_copy(
            src_ref=src.at[to], dst_ref=dst.at[me], send_sem=send_sems.at[which],
            recv_sem=recv_sems.at[which], device_id={"seq": to}, device_id_type=MESH,
        )

    def spread(step):
        return pltpu.make_async_remote_copy(
            src_ref=finals.at[mine], dst_ref=finals.at[mine], send_sem=send_sems.at[2],
            recv_sem=recv_sems.at[2], device_id={"head": lax.rem(mine + step, n_head)},
            device_id_type=MESH,
        )

    def arrived(dst, which, count):
        part = dst.at[pl.ds(0, count)]
        pltpu.make_async_copy(part, part, recv_sems.at[which]).wait()

    def left(src, which, count):
        part = src.at[pl.ds(0, count)]
        pltpu.make_async_copy(part, part, send_sems.at[which]).wait()

    @pl.loop(1, n_seq)
    def _(step):
        exchange(own, gathered, 0, step).start()

    def attend(block, carry):
        part = rows(block * BLOCK, BLOCK)
        queries, vals = q[part, :], v[part, :]
        scores = lax.dot_general(
            queries, k[part, :], (((1,), (1,)), ((), ())), preferred_element_type=F32
        )
        weights = (scores * within[...]).astype(BF16)
        local = jnp.dot(weights, vals, preferred_element_type=F32)
        inter = jnp.dot(
            jnp.concatenate([queries, queries], axis=1),
            jnp.concatenate(split(before[block]), axis=0),
            preferred_element_type=F32,
        )
        raw[part, :] = local + lead[...] * inter
        return carry

    @pl.loop(0, PIECES)
    def _(piece):
        load(2, piece).wait()

    first = blocks * FIRST // 32
    lax.fori_loop(0, first, attend, 0)

    arrived(gathered, 0, n_seq - 1)

    def advance(step, state):
        prefix[step] = state
        return state * whole + gathered[step]

    finals[mine] = lax.fori_loop(
        0, n_seq, advance, jnp.zeros(gathered.shape[1:], F32)
    )
    landed[me] = prefix[me]

    @pl.loop(1, n_seq)
    def _(step):
        exchange(prefix, landed, 1, step).start()

    @pl.loop(1, n_head)
    def _(step):
        spread(step).start()

    lax.fori_loop(first, blocks, attend, 0)

    read_gain.wait()
    arrived(finals, 2, n_head - 1)
    final[...] = finals[...]
    arrived(landed, 1, n_seq - 1)
    high, low = split(landed[...].reshape(width, width))
    prior[:width, :] = high
    prior[width:, :] = low
    left(own, 0, n_seq - 1)
    left(prefix, 1, n_seq - 1)
    left(finals, 2, n_head - 1)


def finish_kernel(
    raw, q, prior, final, lead, gain, decay, out_hbm, final_out, out, sems, final_sem
):
    tokens, width = q.shape
    blocks = tokens // BLOCK
    per_piece = blocks // PIECES
    piece_rows = per_piece * BLOCK

    def write(piece):
        part = rows(piece * piece_rows, piece_rows)
        return pltpu.make_async_copy(out.at[part], out_hbm.at[part], sems.at[piece])

    write_final = pltpu.make_async_copy(final, final_out, final_sem.at[0])
    write_final.start()

    def finish(piece, ahead):
        for j in range(per_piece):
            part = rows((piece * per_piece + j) * BLOCK, BLOCK)
            queries = q[part, :]
            inter = jnp.dot(
                jnp.concatenate([queries, queries], axis=1), prior[...], preferred_element_type=F32
            )
            value = raw[part, :] + (lead[...] * ahead) * inter
            mean_sq = jnp.mean(value * value, axis=-1, keepdims=True)
            out[part, :] = (value * lax.rsqrt(mean_sq + 1e-06) * gain[...]).astype(BF16)
            ahead = ahead * decay[...]
        write(piece).start()
        return ahead

    lax.fori_loop(0, PIECES, finish, jnp.ones((1, width), F32))

    @pl.loop(0, PIECES)
    def _(piece):
        write(piece).wait()

    write_final.wait()


def on_device(n_seq, n_head, queries, keys, values, exponents, gain):
    tokens, width = queries.shape
    share = width // n_seq
    vmem = pl.BlockSpec(memory_space=pltpu.VMEM)
    anywhere = pl.BlockSpec(memory_space=pl.ANY)
    hbm = pl.BlockSpec(memory_space=pltpu.HBM)
    blocks = tokens // BLOCK
    kept = pl.pallas_call(
        functools.partial(state_kernel, n_seq, n_head),
        out_shape=(
            pltpu.VMEM((tokens, width), F32),
            pltpu.VMEM((tokens, width), BF16),
            pltpu.VMEM((2 * width, width), BF16),
            pltpu.VMEM((n_head, share, width), F32),
            pltpu.VMEM((BLOCK, width), F32),
            pltpu.VMEM((1, width), F32),
            pltpu.VMEM((1, width), F32),
        ),
        in_specs=[anywhere] + [hbm] * 4,
        out_specs=(vmem,) * 7,
        scratch_shapes=[
            pltpu.VMEM((tokens, width), BF16),
            pltpu.VMEM((tokens, width), BF16),
            pltpu.SMEM((1,), jnp.int32),
            pltpu.VMEM((BLOCK, BLOCK), F32),
            pltpu.VMEM((BLOCK, width), F32),
            pltpu.VMEM((blocks, width, width), F32),
            pltpu.VMEM((n_seq, share, width), F32),
            pltpu.VMEM((n_seq, share, width), F32),
            pltpu.VMEM((n_seq, share, width), F32),
            pltpu.VMEM((n_seq, share, width), F32),
            pltpu.VMEM((n_head, share, width), F32),
            pltpu.SemaphoreType.DMA((3, PIECES)),
            pltpu.SemaphoreType.DMA((2,)),
            pltpu.SemaphoreType.DMA((3,)),
            pltpu.SemaphoreType.DMA((3,)),
        ],
        compiler_params=pltpu.CompilerParams(
            collective_id=0, has_side_effects=True, vmem_limit_bytes=32 * 1024 * 1024
        ),
        name="state",
    )(exponents, *(
        pltpu.with_memory_space_constraint(array, pltpu.HBM)
        for array in (gain.reshape(1, width), queries, keys, values)
    ))
    return pl.pallas_call(
        finish_kernel,
        out_shape=(
            jax.ShapeDtypeStruct((tokens, width), BF16),
            jax.ShapeDtypeStruct((n_head, share, width), F32),
        ),
        in_specs=[vmem] * 7,
        out_specs=(anywhere, anywhere),
        scratch_shapes=[
            pltpu.VMEM((tokens, width), BF16),
            pltpu.SemaphoreType.DMA((PIECES,)),
            pltpu.SemaphoreType.DMA((1,)),
        ],
        compiler_params=pltpu.CompilerParams(vmem_limit_bytes=32 * 1024 * 1024),
        name="finish",
    )(*kept)


def solution(mesh):
    return jax.shard_map(
        functools.partial(on_device, mesh.shape["seq"], mesh.shape["head"]),
        mesh=mesh,
        in_specs=(P("seq", "head"), P("seq", "head"), P("seq", "head"), P("head"), P("head")),
        out_specs=(P("seq", "head"), P(None, "seq", None)),
        check_vma=False,
    )
```

```python
import functools

import jax
import jax.numpy as jnp
from jax import lax
from jax.experimental import pallas as pl
from jax.experimental.pallas import tpu as pltpu
from jax.sharding import PartitionSpec as P

BLOCK = 256
PIECES = 4
MESH = pl.DeviceIdType.MESH
F32 = jnp.float32
BF16 = jnp.bfloat16


def rows(start, count):
    return pl.ds(pl.multiple_of(start, count), count)


def split(value):
    high = value.astype(BF16)
    return high, (value - high.astype(F32)).astype(BF16)


def state_kernel(
    n_seq, n_head,
    exps_hbm, gain_hbm, q_hbm, k_hbm, v_hbm,
    out, final,
    q, k, v, raw, exps, gain, within, lead, tail, before, own, gathered, prefix, landed,
    last, finals, in_sems, small_sems, send_sems, recv_sems, ready,
):
    me, mine = lax.axis_index("seq"), lax.axis_index("head")
    n_hubs = n_seq // 2
    half = n_hubs // 2
    ring = min(4, half)
    is_hub = me < n_hubs
    hub_count = is_hub.astype(jnp.int32)
    my_chip = me // 2
    my_hub = 2 * lax.rem(my_chip, half) + my_chip // half
    chip = jnp.minimum(me // 2 + half * lax.rem(me, 2), n_hubs - 1)
    tokens, width = q.shape
    blocks = tokens // BLOCK
    per_piece = blocks // PIECES
    piece_rows = per_piece * BLOCK

    def load(which, piece):
        src, dst = ((k_hbm, k), (v_hbm, v), (q_hbm, q))[which]
        part = rows(piece * piece_rows, piece_rows)
        return pltpu.make_async_copy(src.at[part], dst.at[part], in_sems.at[which, piece])

    read_exps = pltpu.make_async_copy(exps_hbm, exps, small_sems.at[0])
    read_gain = pltpu.make_async_copy(gain_hbm, gain, small_sems.at[1])
    read_exps.start()
    for piece in range(PIECES):
        load(0, piece).start()
        load(1, piece).start()
    read_gain.start()

    barrier = pltpu.get_barrier_semaphore()

    def signal(sem, seq, head):
        pl.semaphore_signal(
            sem, inc=1, device_id={"seq": seq, "head": head}, device_id_type=MESH
        )

    @pl.when(is_hub)
    def _():
        @pl.loop(1, n_seq)
        def _(step):
            signal(barrier, lax.rem(me + step, n_seq), mine)

        @pl.loop(mine + 1, n_head)
        def _(head):
            signal(barrier, 2 * chip, head)
            signal(barrier, 2 * chip + 1, head)

    @pl.loop(mine + 1, n_head)
    def _(head):
        signal(barrier, my_hub, head)

    read_exps.wait()
    rate = exps[0].astype(F32) / 16777216.0
    row = lax.broadcasted_iota(jnp.int32, (BLOCK, width), 0).astype(F32)
    lead[...] = jnp.exp2(-rate * (row + 1.0))
    tail[...] = jnp.exp2(-rate * (BLOCK - 1.0 - row))
    gap = (
        lax.broadcasted_iota(jnp.int32, (BLOCK, BLOCK), 0)
        - lax.broadcasted_iota(jnp.int32, (BLOCK, BLOCK), 1)
    ).astype(F32)
    within[...] = jnp.where(gap >= 0.0, jnp.exp2(-rate * jnp.maximum(gap, 0.0)), 0.0)
    ones = jnp.ones((1, width), F32)
    decay = jnp.exp2(-rate * BLOCK * ones)
    whole = jnp.exp2(-rate * tokens * ones)

    def contribute(piece, state):
        load(0, piece).wait()
        load(1, piece).wait()
        for j in range(per_piece):
            block = piece * per_piece + j
            part = rows(block * BLOCK, BLOCK)
            scaled = (k[part, :].astype(F32) * tail[...]).astype(BF16)
            term = lax.dot_general(
                scaled, v[part, :], (((0,), (0,)), ((), ())), preferred_element_type=F32
            )
            before[block] = state
            state = state * decay + term
        return state

    total = lax.fori_loop(0, PIECES, contribute, jnp.zeros((width, width), F32))
    own[...] = total.reshape(own.shape)
    for piece in range(PIECES):
        load(2, piece).start()

    pl.semaphore_wait(barrier, n_hubs - hub_count + mine * (1 + 2 * hub_count))

    def contribution(to, to_chip):
        return pltpu.make_async_remote_copy(
            src_ref=own.at[to_chip], dst_ref=gathered.at[me], send_sem=send_sems.at[0],
            recv_sem=recv_sems.at[0], device_id={"seq": to, "head": mine}, device_id_type=MESH,
        )

    def entering(to):
        return pltpu.make_async_remote_copy(
            src_ref=prefix.at[to], dst_ref=landed.at[chip], send_sem=send_sems.at[1],
            recv_sem=recv_sems.at[1], device_id={"seq": to, "head": mine}, device_id_type=MESH,
        )

    def ending(core, head):
        return pltpu.make_async_remote_copy(
            src_ref=last.at[core], dst_ref=finals.at[mine], send_sem=send_sems.at[2],
            recv_sem=recv_sems.at[2], device_id={"seq": 2 * chip + core, "head": head},
            device_id_type=MESH,
        )

    def drain(sem, ref, count):
        part = ref.at[pl.ds(0, count)]
        pltpu.make_async_copy(part, part, sem).wait()

    across = lax.rem(my_chip, ring)
    for offset in sorted(range(ring), key=lambda d: -min(d, ring - d)):
        for start in range(0, half, ring):
            for core in range(2):
                spot = start + lax.rem(across + offset, ring)
                to = 2 * spot + core

                @pl.when(to != me)
                def _():
                    contribution(to, spot + half * core).start()

    @pl.loop(0, mine)
    def _(head):
        signal(ready, my_hub, head)

    def attend(block, carry):
        part = rows(block * BLOCK, BLOCK)
        queries, vals = q[part, :], v[part, :]
        scores = lax.dot_general(
            queries, k[part, :], (((1,), (1,)), ((), ())), preferred_element_type=F32
        )
        weights = (scores * within[...]).astype(BF16)
        local = jnp.dot(weights, vals, preferred_element_type=F32)
        inter = jnp.dot(
            jnp.concatenate([queries, queries], axis=1),
            jnp.concatenate(split(before[block]), axis=0),
            preferred_element_type=F32,
        )
        raw[part, :] = local + lead[...] * inter
        return carry

    for piece in range(PIECES):
        load(2, piece).wait()
    first = blocks * 3 // 4
    lax.fori_loop(0, first, attend, 0, unroll=min(8, first))

    @pl.when(is_hub)
    def _():
        gathered[me] = own[chip]
        drain(recv_sems.at[0], gathered, n_seq - 1)
        state = jnp.zeros(gathered.shape[1:], F32)
        for step in range(n_seq):
            prefix[step] = state
            state = state * whole + gathered[step]
        last[...] = state.reshape(last.shape)

        @pl.when(2 * chip == me)
        def _():
            finals[mine] = last[0]

        @pl.loop(0, mine)
        def _(head):
            ending(0, head).start()
            ending(1, head).start()

        @pl.when(2 * chip != me)
        def _():
            ending(0, mine).start()

        ending(1, mine).start()
        landed[chip] = prefix[me]

        @pl.loop(1, n_hubs)
        def _(step):
            entering(lax.rem(me + step, n_hubs)).start()

        @pl.loop(0, n_hubs)
        def _(step):
            entering(n_hubs + lax.rem(me + step, n_hubs)).start()

        @pl.when(mine < n_head - 1)
        def _():
            pl.semaphore_wait(ready, 2 * (n_head - 1 - mine))

        @pl.loop(mine + 1, n_head)
        def _(head):
            ending(0, head).start()
            ending(1, head).start()

    lax.fori_loop(first, blocks, attend, 0, unroll=min(8, blocks - first))
    read_gain.wait()

    @pl.when(is_hub)
    def _():
        drain(recv_sems.at[1], landed, n_hubs - 1)

    @pl.when(jnp.logical_not(is_hub))
    def _():
        drain(recv_sems.at[1], landed, n_hubs)

    prior = jnp.concatenate(split(landed[...].reshape(width, width)), axis=0)

    def finish(piece, ahead):
        for j in range(per_piece):
            part = rows((piece * per_piece + j) * BLOCK, BLOCK)
            queries = q[part, :]
            inter = jnp.dot(
                jnp.concatenate([queries, queries], axis=1), prior, preferred_element_type=F32
            )
            value = raw[part, :] + (lead[...] * ahead) * inter
            mean_sq = jnp.mean(value * value, axis=-1, keepdims=True)
            out[part, :] = (value * lax.rsqrt(mean_sq + 1e-06) * gain[...]).astype(BF16)
            ahead = ahead * decay
        return ahead

    lax.fori_loop(0, PIECES, finish, ones)

    @pl.when(is_hub)
    def _():
        drain(send_sems.at[0], own, n_hubs - 1)
        drain(send_sems.at[1], prefix, n_seq - 1)

        @pl.when(2 * chip == me)
        def _():
            drain(send_sems.at[2], finals.at[pl.ds(0, n_head - 1)], n_head - 1)

        @pl.when(2 * chip != me)
        def _():
            drain(send_sems.at[2], finals, n_head)

        drain(send_sems.at[2], finals, n_head)

    @pl.when(jnp.logical_not(is_hub))
    def _():
        drain(send_sems.at[0], own, n_hubs)

    @pl.when(my_hub == me)
    def _():
        drain(recv_sems.at[2], finals, n_head - 1)

    @pl.when(my_hub != me)
    def _():
        drain(recv_sems.at[2], finals, n_head)

    final[...] = finals[...]


def write_kernel(out, final, out_hbm, final_hbm, sems):
    piece_rows = out.shape[0] // PIECES
    copies = [pltpu.make_async_copy(final, final_hbm, sems.at[PIECES])]
    for piece in range(PIECES):
        part = pl.ds(piece * piece_rows, piece_rows)
        copies.append(pltpu.make_async_copy(out.at[part], out_hbm.at[part], sems.at[piece]))
    for copy in copies:
        copy.start()
    for copy in copies:
        copy.wait()


def on_device(n_seq, n_head, queries, keys, values, exponents, gain):
    tokens, width = queries.shape
    share = width // n_seq
    n_hubs = n_seq // 2
    vmem = pl.BlockSpec(memory_space=pltpu.VMEM)
    anywhere = pl.BlockSpec(memory_space=pl.ANY)
    hbm = pl.BlockSpec(memory_space=pltpu.HBM)
    blocks = tokens // BLOCK
    kept = pl.pallas_call(
        functools.partial(state_kernel, n_seq, n_head),
        out_shape=(
            pltpu.VMEM((tokens, width), BF16),
            pltpu.VMEM((n_head, share, width), F32),
        ),
        in_specs=[anywhere] + [hbm] * 4,
        out_specs=(vmem,) * 2,
        scratch_shapes=[
            pltpu.VMEM((tokens, width), BF16),
            pltpu.VMEM((tokens, width), BF16),
            pltpu.VMEM((tokens, width), BF16),
            pltpu.VMEM((tokens, width), F32),
            pltpu.SMEM((1,), jnp.int32),
            pltpu.VMEM((1, width), F32),
            pltpu.VMEM((BLOCK, BLOCK), F32),
            pltpu.VMEM((BLOCK, width), F32),
            pltpu.VMEM((BLOCK, width), F32),
            pltpu.VMEM((blocks, width, width), F32),
            pltpu.VMEM((n_hubs, 2 * share, width), F32),
            pltpu.VMEM((n_seq, 2 * share, width), F32),
            pltpu.VMEM((n_seq, 2 * share, width), F32),
            pltpu.VMEM((n_hubs, 2 * share, width), F32),
            pltpu.VMEM((2, share, width), F32),
            pltpu.VMEM((n_head, share, width), F32),
            pltpu.SemaphoreType.DMA((3, PIECES)),
            pltpu.SemaphoreType.DMA((2,)),
            pltpu.SemaphoreType.DMA((3,)),
            pltpu.SemaphoreType.DMA((3,)),
            pltpu.SemaphoreType.REGULAR,
        ],
        compiler_params=pltpu.CompilerParams(
            collective_id=0, has_side_effects=True, vmem_limit_bytes=40 * 1024 * 1024
        ),
        name="state",
    )(exponents, *(
        pltpu.with_memory_space_constraint(array, pltpu.HBM)
        for array in (gain.reshape(1, width), queries, keys, values)
    ))
    return pl.pallas_call(
        write_kernel,
        out_shape=(
            jax.ShapeDtypeStruct((tokens, width), BF16),
            jax.ShapeDtypeStruct((n_head, share, width), F32),
        ),
        in_specs=[vmem] * 2,
        out_specs=(anywhere, anywhere),
        scratch_shapes=[pltpu.SemaphoreType.DMA((PIECES + 1,))],
        compiler_params=pltpu.CompilerParams(vmem_limit_bytes=32 * 1024 * 1024),
        name="write",
    )(*kept)


def solution(mesh):
    return jax.shard_map(
        functools.partial(on_device, mesh.shape["seq"], mesh.shape["head"]),
        mesh=mesh,
        in_specs=(P("seq", "head"), P("seq", "head"), P("seq", "head"), P("head"), P("head")),
        out_specs=(P("seq", "head"), P(None, "seq", None)),
        check_vma=False,
    )
```

```python
import functools

import jax
import jax.numpy as jnp
from jax import lax
from jax.experimental import pallas as pl
from jax.experimental.pallas import tpu as pltpu
from jax.sharding import PartitionSpec as P

BLOCK = 256
PIECES = 4
EARLY = 1
MESH = pl.DeviceIdType.MESH
F32 = jnp.float32
BF16 = jnp.bfloat16


def rows(start, count):
    return pl.ds(pl.multiple_of(start, count), count)


def split(value):
    high = value.astype(BF16)
    return high, (value - high.astype(F32)).astype(BF16)


def state_kernel(
    n_seq, n_head,
    exps_hbm, gain_hbm, q_hbm, k_hbm, v_hbm,
    out, final,
    q, k, v, raw, exps, gain, within, lead, tail, before, own, gathered, prefix, landed,
    last, finals, toward, direct, in_sems, small_sems, send_sems, recv_sems, ready,
):
    me, mine = lax.axis_index("seq"), lax.axis_index("head")
    n_hubs = n_seq // 2
    half = n_hubs // 2
    ring = min(4, half)
    is_hub = me < n_hubs
    hub_count = is_hub.astype(jnp.int32)
    my_chip = me // 2
    my_hub = 2 * lax.rem(my_chip, half) + my_chip // half
    chip = jnp.minimum(me // 2 + half * lax.rem(me, 2), n_hubs - 1)
    tokens, width = q.shape
    blocks = tokens // BLOCK
    cuts = [blocks * part // 16 for part in (0, 5, 10, 14, 16)]
    share = width // n_seq
    far = n_head // 2
    is_far = mine >= far
    is_early = jnp.logical_and(me == EARLY, mine == 0)

    skip = jnp.logical_and(chip == EARLY // 2, is_far)

    def load(which, piece):
        src, dst = ((k_hbm, k), (v_hbm, v), (q_hbm, q))[which]
        part = pl.ds(cuts[piece] * BLOCK, (cuts[piece + 1] - cuts[piece]) * BLOCK)
        return pltpu.make_async_copy(src.at[part], dst.at[part], in_sems.at[which, piece])

    read_exps = pltpu.make_async_copy(exps_hbm, exps, small_sems.at[0])
    read_gain = pltpu.make_async_copy(gain_hbm, gain, small_sems.at[1])
    read_exps.start()
    for piece in range(PIECES):
        load(0, piece).start()
        load(1, piece).start()
    read_gain.start()

    barrier = pltpu.get_barrier_semaphore()

    def signal(sem, seq, head):
        pl.semaphore_signal(
            sem, inc=1, device_id={"seq": seq, "head": head}, device_id_type=MESH
        )

    @pl.when(is_hub)
    def _():
        @pl.loop(1, n_seq)
        def _(step):
            signal(barrier, lax.rem(me + step, n_seq), mine)

        @pl.loop(mine + 1, n_head)
        def _(head):
            signal(barrier, 2 * chip, head)
            signal(barrier, 2 * chip + 1, head)

    @pl.loop(mine + 1, n_head)
    def _(head):
        signal(barrier, my_hub, head)

    @pl.when(is_early)
    def _():
        @pl.loop(far, n_head)
        def _(head):
            @pl.loop(0, n_seq)
            def _(seq):
                signal(barrier, seq, head)

    read_exps.wait()
    rate = exps[0].astype(F32) / 16777216.0
    row = lax.broadcasted_iota(jnp.int32, (BLOCK, width), 0).astype(F32)
    tail[...] = jnp.exp2(-rate * (BLOCK - 1.0 - row))
    ones = jnp.ones((1, width), F32)
    decay = jnp.exp2(-rate * BLOCK * ones)
    whole = jnp.exp2(-rate * tokens * ones)

    total = jnp.zeros((width, width), F32)
    for piece in range(PIECES):
        load(0, piece).wait()
        load(1, piece).wait()
        for block in range(cuts[piece], cuts[piece + 1]):
            part = pl.ds(block * BLOCK, BLOCK)
            scaled = (k[part, :].astype(F32) * tail[...]).astype(BF16)
            term = lax.dot_general(
                scaled, v[part, :], (((0,), (0,)), ((), ())), preferred_element_type=F32
            )
            before[block] = total
            total = total * decay + term
    own[...] = total.reshape(own.shape)
    left = (n_seq - 1 - me).astype(F32) * tokens
    toward[...] = total[EARLY * share:(EARLY + 1) * share, :] * jnp.exp2(-rate * left * ones)

    pl.semaphore_wait(
        barrier, n_hubs - hub_count + mine * (1 + 2 * hub_count) + is_far.astype(jnp.int32)
    )

    def contribution(to, to_chip):
        return pltpu.make_async_remote_copy(
            src_ref=own.at[to_chip], dst_ref=gathered.at[me], send_sem=send_sems.at[0],
            recv_sem=recv_sems.at[hub_count], device_id={"seq": to, "head": mine}, device_id_type=MESH,
        )

    def entering(to):
        return pltpu.make_async_remote_copy(
            src_ref=prefix.at[to], dst_ref=landed.at[chip], send_sem=send_sems.at[1],
            recv_sem=recv_sems.at[2], device_id={"seq": to, "head": mine}, device_id_type=MESH,
        )

    def ending(core, head):
        return pltpu.make_async_remote_copy(
            src_ref=last.at[core], dst_ref=finals.at[mine], send_sem=send_sems.at[2],
            recv_sem=recv_sems.at[3], device_id={"seq": 2 * chip + core, "head": head},
            device_id_type=MESH,
        )

    to_early = pltpu.make_async_remote_copy(
        src_ref=toward, dst_ref=direct.at[jnp.maximum(mine - far, 0), me], send_sem=send_sems.at[3],
        recv_sem=recv_sems.at[4], device_id={"seq": EARLY, "head": 0}, device_id_type=MESH,
    )

    @pl.when(is_far)
    def _():
        to_early.start()

    def drain(sem, ref, count):
        part = ref.at[pl.ds(0, count)]
        pltpu.make_async_copy(part, part, sem).wait()

    across = lax.rem(my_chip, ring)
    for offset in sorted(range(ring), key=lambda d: -min(d, ring - d)):
        for start in range(0, half, ring):
            for core in range(2):
                spot = start + lax.rem(across + offset, ring)
                to = 2 * spot + core

                @pl.when(to != me)
                def _():
                    contribution(to, spot + half * core).start()

    @pl.loop(0, mine)
    def _(head):
        signal(ready, my_hub, head)

    for piece in range(PIECES):
        load(2, piece).start()
    lead[...] = jnp.exp2(-rate * (row + 1.0))
    gap = (
        lax.broadcasted_iota(jnp.int32, (BLOCK, BLOCK), 0)
        - lax.broadcasted_iota(jnp.int32, (BLOCK, BLOCK), 1)
    ).astype(F32)
    within[...] = jnp.where(gap >= 0.0, jnp.exp2(-rate * jnp.maximum(gap, 0.0)), 0.0)

    def attend(block, carry):
        part = rows(block * BLOCK, BLOCK)
        queries, vals = q[part, :], v[part, :]
        scores = lax.dot_general(
            queries, k[part, :], (((1,), (1,)), ((), ())), preferred_element_type=F32
        )
        weights = (scores * within[...]).astype(BF16)
        local = jnp.dot(weights, vals, preferred_element_type=F32)
        inter = jnp.dot(
            jnp.concatenate([queries, queries], axis=1),
            jnp.concatenate(split(before[block]), axis=0),
            preferred_element_type=F32,
        )
        raw[part, :] = local + lead[...] * inter
        return carry

    for piece in range(PIECES):
        load(2, piece).wait()
    first = blocks * 3 // 4
    lax.fori_loop(0, first, attend, 0, unroll=min(8, first))

    @pl.when(is_hub)
    def _():
        gathered[me] = own[chip]
        drain(recv_sems.at[1], gathered, n_hubs - 1)
        state = jnp.zeros(gathered.shape[1:], F32)
        for step in range(n_seq):
            if step == n_hubs:
                drain(recv_sems.at[0], gathered, n_seq - n_hubs)
            prefix[step] = state
            state = state * whole + gathered[step]
        last[...] = state.reshape(last.shape)

        @pl.when(2 * chip == me)
        def _():
            finals[mine] = last[0]

        @pl.loop(0, mine)
        def _(head):
            @pl.when(jnp.logical_not(jnp.logical_and(skip, head == 0)))
            def _():
                ending(EARLY % 2, head).start()

            ending(1 - EARLY % 2, head).start()

        @pl.when(2 * chip != me)
        def _():
            ending(0, mine).start()

        ending(1, mine).start()
        landed[chip] = prefix[me]

        @pl.loop(1, n_hubs)
        def _(step):
            entering(lax.rem(me + step, n_hubs)).start()

        @pl.loop(0, n_hubs)
        def _(step):
            entering(n_hubs + lax.rem(me + step, n_hubs)).start()

        @pl.when(mine < n_head - 1)
        def _():
            pl.semaphore_wait(ready, 2 * (n_head - 1 - mine))

        @pl.loop(mine + 1, n_head)
        def _(head):
            ending(0, head).start()
            ending(1, head).start()

    lax.fori_loop(first, blocks, attend, 0, unroll=min(8, blocks - first))
    read_gain.wait()

    @pl.when(is_hub)
    def _():
        drain(recv_sems.at[2], landed, n_hubs - 1)

    @pl.when(jnp.logical_not(is_hub))
    def _():
        drain(recv_sems.at[2], landed, n_hubs)

    prior = jnp.concatenate(split(landed[...].reshape(width, width)), axis=0)

    def finish(piece, ahead):
        for j in range(blocks // 2):
            part = rows((piece * (blocks // 2) + j) * BLOCK, BLOCK)
            queries = q[part, :]
            inter = jnp.dot(
                jnp.concatenate([queries, queries], axis=1), prior, preferred_element_type=F32
            )
            value = raw[part, :] + (lead[...] * ahead) * inter
            mean_sq = jnp.mean(value * value, axis=-1, keepdims=True)
            out[part, :] = (value * lax.rsqrt(mean_sq + 1e-06) * gain[...]).astype(BF16)
            ahead = ahead * decay
        return ahead

    lax.fori_loop(0, 2, finish, ones)

    @pl.when(is_hub)
    def _():
        drain(send_sems.at[0], own, n_hubs - 1)
        drain(send_sems.at[1], prefix, n_seq - 1)

        @pl.when(2 * chip == me)
        def _():
            drain(send_sems.at[2], finals, n_head - 1)

        @pl.when(2 * chip != me)
        def _():
            drain(send_sems.at[2], finals, n_head)

        @pl.when(skip)
        def _():
            drain(send_sems.at[2], finals, n_head - 1)

        @pl.when(jnp.logical_not(skip))
        def _():
            drain(send_sems.at[2], finals, n_head)

    @pl.when(jnp.logical_not(is_hub))
    def _():
        drain(send_sems.at[0], own, n_hubs)

    @pl.when(is_far)
    def _():
        to_early.wait_send()

    @pl.when(is_early)
    def _():
        drain(recv_sems.at[3], finals, far)
        pltpu.make_async_copy(direct, direct, recv_sems.at[4]).wait()
        for head in range(far, n_head):
            finals[head] = jnp.sum(direct[head - far], axis=0)

    @pl.when(jnp.logical_and(my_hub == me, jnp.logical_not(is_early)))
    def _():
        drain(recv_sems.at[3], finals, n_head - 1)

    @pl.when(jnp.logical_and(my_hub != me, jnp.logical_not(is_early)))
    def _():
        drain(recv_sems.at[3], finals, n_head)

    final[...] = finals[...]


def write_kernel(out, final, out_hbm, final_hbm, sems):
    piece_rows = out.shape[0] // PIECES
    copies = [pltpu.make_async_copy(final, final_hbm, sems.at[PIECES])]
    for piece in range(PIECES):
        part = pl.ds(piece * piece_rows, piece_rows)
        copies.append(pltpu.make_async_copy(out.at[part], out_hbm.at[part], sems.at[piece]))
    for copy in copies:
        copy.start()
    for copy in copies:
        copy.wait()


def on_device(n_seq, n_head, queries, keys, values, exponents, gain):
    tokens, width = queries.shape
    share = width // n_seq
    n_hubs = n_seq // 2
    vmem = pl.BlockSpec(memory_space=pltpu.VMEM)
    anywhere = pl.BlockSpec(memory_space=pl.ANY)
    hbm = pl.BlockSpec(memory_space=pltpu.HBM)
    blocks = tokens // BLOCK
    kept = pl.pallas_call(
        functools.partial(state_kernel, n_seq, n_head),
        out_shape=(
            pltpu.VMEM((tokens, width), BF16),
            pltpu.VMEM((n_head, share, width), F32),
        ),
        in_specs=[anywhere] + [hbm] * 4,
        out_specs=(vmem,) * 2,
        scratch_shapes=[
            pltpu.VMEM((tokens, width), BF16),
            pltpu.VMEM((tokens, width), BF16),
            pltpu.VMEM((tokens, width), BF16),
            pltpu.VMEM((tokens, width), F32),
            pltpu.SMEM((1,), jnp.int32),
            pltpu.VMEM((1, width), F32),
            pltpu.VMEM((BLOCK, BLOCK), F32),
            pltpu.VMEM((BLOCK, width), F32),
            pltpu.VMEM((BLOCK, width), F32),
            pltpu.VMEM((blocks, width, width), F32),
            pltpu.VMEM((n_hubs, 2 * share, width), F32),
            pltpu.VMEM((n_seq, 2 * share, width), F32),
            pltpu.VMEM((n_seq, 2 * share, width), F32),
            pltpu.VMEM((n_hubs, 2 * share, width), F32),
            pltpu.VMEM((2, share, width), F32),
            pltpu.VMEM((n_head, share, width), F32),
            pltpu.VMEM((share, width), F32),
            pltpu.VMEM((n_head - n_head // 2, n_seq, share, width), F32),
            pltpu.SemaphoreType.DMA((3, PIECES)),
            pltpu.SemaphoreType.DMA((2,)),
            pltpu.SemaphoreType.DMA((4,)),
            pltpu.SemaphoreType.DMA((5,)),
            pltpu.SemaphoreType.REGULAR,
        ],
        compiler_params=pltpu.CompilerParams(
            collective_id=0, has_side_effects=True, vmem_limit_bytes=40 * 1024 * 1024
        ),
        name="state",
    )(exponents, *(
        pltpu.with_memory_space_constraint(array, pltpu.HBM)
        for array in (gain.reshape(1, width), queries, keys, values)
    ))
    return pl.pallas_call(
        write_kernel,
        out_shape=(
            jax.ShapeDtypeStruct((tokens, width), BF16),
            jax.ShapeDtypeStruct((n_head, share, width), F32),
        ),
        in_specs=[vmem] * 2,
        out_specs=(anywhere, anywhere),
        scratch_shapes=[pltpu.SemaphoreType.DMA((PIECES + 1,))],
        compiler_params=pltpu.CompilerParams(vmem_limit_bytes=32 * 1024 * 1024),
        name="write",
    )(*kept)


def solution(mesh):
    return jax.shard_map(
        functools.partial(on_device, mesh.shape["seq"], mesh.shape["head"]),
        mesh=mesh,
        in_specs=(P("seq", "head"), P("seq", "head"), P("seq", "head"), P("head"), P("head")),
        out_specs=(P("seq", "head"), P(None, "seq", None)),
        check_vma=False,
    )
```

```python
import functools

import jax
import jax.numpy as jnp
from jax import lax
from jax.experimental import pallas as pl
from jax.experimental.pallas import tpu as pltpu
from jax.sharding import PartitionSpec as P

BLOCK = 256
PIECES = 4
EARLY = 1
TURN = 2
MESH = pl.DeviceIdType.MESH
F32 = jnp.float32
BF16 = jnp.bfloat16


def hub_chips(chips):
    if chips == 16:
        return ((0, 7), (1, 6), (2, 14), (3, 11), (4, 9), (5, 10), (8, 13), (12, 15))
    return tuple((chip, chips - 1 - chip) for chip in range(chips // 2))


def pick(index, table):
    value = jnp.int32(table[0])
    for entry in range(1, len(table)):
        value = jnp.where(index == entry, jnp.int32(table[entry]), value)
    return value


def rows(start, count):
    return pl.ds(pl.multiple_of(start, count), count)


def split(value):
    high = value.astype(BF16)
    return high, (value - high.astype(F32)).astype(BF16)


def state_kernel(
    n_seq, n_head,
    exps_hbm, gain_hbm, q_hbm, k_hbm, v_hbm,
    out, final,
    q, k, v, raw, exps, gain, within, lead, tail, before, own, gathered, prefix, landed,
    last, finals, toward, direct, in_sems, small_sems, send_sems, recv_sems, ready,
):
    me, mine = lax.axis_index("seq"), lax.axis_index("head")
    n_hubs = n_seq // 4
    tokens, width = q.shape
    blocks = tokens // BLOCK
    cuts = [blocks * part // 16 for part in (0, 5, 10, 14, 16)]
    share = width // n_seq
    def load(which, piece):
        src, dst = ((k_hbm, k), (v_hbm, v))[which]
        part = pl.ds(cuts[piece] * BLOCK, (cuts[piece + 1] - cuts[piece]) * BLOCK)
        return pltpu.make_async_copy(src.at[part], dst.at[part], in_sems.at[which, piece])

    read_exps = pltpu.make_async_copy(exps_hbm, exps, small_sems.at[0])
    read_q = pltpu.make_async_copy(q_hbm, q, in_sems.at[2, 0])
    read_gain = pltpu.make_async_copy(gain_hbm, gain, small_sems.at[1])
    read_exps.start()
    for piece in range(PIECES):
        load(0, piece).start()
        load(1, piece).start()
    read_gain.start()

    seats = hub_chips(2 * n_hubs)
    seat_spots = {chip: spot for spot, pair in enumerate(seats) for chip in pair}
    my_spot = pick(me // 2, [seat_spots[chip] for chip in range(2 * n_hubs)])
    other = pick(my_spot, [pair[1] for pair in seats])
    home = 2 * pick(my_spot, [pair[0] for pair in seats]) + 1
    core = lax.rem(me, 2)
    targets = (me, 2 * (me // 2) + 1 - core, 2 * other + 1, 2 * other)

    def hub(first, head):
        return first - jnp.logical_and(first == EARLY, head == 0).astype(jnp.int32)

    is_hub = hub(home, mine) == me
    hub_count = is_hub.astype(jnp.int32)
    far = n_head // 2
    is_far = mine >= far
    skip = jnp.logical_and(me == EARLY, is_far)
    is_early = jnp.logical_and(me == EARLY, mine == 0)
    quarter = n_seq // 4

    barrier = pltpu.get_barrier_semaphore()

    def signal(sem, seq, head):
        pl.semaphore_signal(
            sem, inc=1, device_id={"seq": seq, "head": head}, device_id_type=MESH
        )

    @pl.when(is_hub)
    def _():
        @pl.loop(0, n_seq)
        def _(step):
            to = n_seq - 1 - step

            @pl.when(to != me)
            def _():
                signal(barrier, to, mine)

        @pl.loop(mine + 1, n_head)
        def _(head):
            for target in targets:
                signal(barrier, target, head)

    @pl.loop(mine + 1, n_head)
    def _(head):
        signal(barrier, hub(home, head), head)

    @pl.when(is_early)
    def _():
        @pl.loop(far, n_head)
        def _(head):
            @pl.loop(0, n_seq)
            def _(seq):
                signal(barrier, seq, head)

    read_exps.wait()
    rate = exps[0].astype(F32) / 16777216.0
    row = lax.broadcasted_iota(jnp.int32, (BLOCK, width), 0).astype(F32)
    tail[...] = jnp.exp2(-rate * (BLOCK - 1.0 - row))
    ones = jnp.ones((1, width), F32)
    decay = jnp.exp2(-rate * BLOCK * ones)
    whole = jnp.exp2(-rate * tokens * ones)

    total = jnp.zeros((width, width), F32)
    for piece in range(PIECES):
        load(0, piece).wait()
        load(1, piece).wait()
        if piece == PIECES - 1:
            read_q.start()
        for block in range(cuts[piece], cuts[piece + 1]):
            part = pl.ds(block * BLOCK, BLOCK)
            scaled = (k[part, :].astype(F32) * tail[...]).astype(BF16)
            term = lax.dot_general(
                scaled, v[part, :], (((0,), (0,)), ((), ())), preferred_element_type=F32
            )
            before[block] = total
            total = total * decay + term
    for spot in range(n_hubs):
        for slot, seat in enumerate(seats[spot]):
            own[spot, 2 * share * slot:2 * share * (slot + 1), :] = (
                total[2 * share * seat:2 * share * (seat + 1), :]
            )
    left = (n_seq - 1 - me).astype(F32) * tokens
    toward[...] = total[EARLY * share:(EARLY + 1) * share, :] * jnp.exp2(-rate * left * ones)

    pl.semaphore_wait(
        barrier, n_hubs - hub_count + mine * (1 + 4 * hub_count) + is_far.astype(jnp.int32)
    )

    def contribution(to, spot):
        return pltpu.make_async_remote_copy(
            src_ref=own.at[spot], dst_ref=gathered.at[me], send_sem=send_sems.at[0],
            recv_sem=recv_sems.at[me // quarter], device_id={"seq": to, "head": mine}, device_id_type=MESH,
        )

    def entering(to):
        return pltpu.make_async_remote_copy(
            src_ref=prefix.at[to], dst_ref=landed.at[my_spot], send_sem=send_sems.at[1],
            recv_sem=recv_sems.at[4], device_id={"seq": to, "head": mine}, device_id_type=MESH,
        )

    def ending(which, head):
        return pltpu.make_async_remote_copy(
            src_ref=last.at[which], dst_ref=finals.at[mine], send_sem=send_sems.at[2],
            recv_sem=recv_sems.at[5], device_id={"seq": targets[which], "head": head},
            device_id_type=MESH,
        )

    to_early = pltpu.make_async_remote_copy(
        src_ref=toward, dst_ref=direct.at[jnp.maximum(mine - far, 0), me], send_sem=send_sems.at[3],
        recv_sem=recv_sems.at[6], device_id={"seq": EARLY, "head": 0}, device_id_type=MESH,
    )

    @pl.when(is_far)
    def _():
        to_early.start()

    def drain(sem, ref, count):
        part = ref.at[pl.ds(0, count)]
        pltpu.make_async_copy(part, part, sem).wait()

    def contribute(order):
        for spot in order:
            to = hub(jnp.int32(2 * seats[spot][0] + 1), mine)

            @pl.when(me != to)
            def _():
                contribution(to, spot).start()

    order = list(range(n_hubs))

    @pl.when(lax.rem(me // 2, 2) == 0)
    def _():
        contribute(order)

    @pl.when(lax.rem(me // 2, 2) == 1)
    def _():
        contribute(order[n_hubs // 2:] + order[:n_hubs // 2])

    @pl.loop(0, mine)
    def _(head):
        signal(ready, hub(home, head), head)

    lead[...] = jnp.exp2(-rate * (row + 1.0))
    gap = (
        lax.broadcasted_iota(jnp.int32, (BLOCK, BLOCK), 0)
        - lax.broadcasted_iota(jnp.int32, (BLOCK, BLOCK), 1)
    ).astype(F32)
    within[...] = jnp.where(gap >= 0.0, jnp.exp2(-rate * jnp.maximum(gap, 0.0)), 0.0)

    def attend(block, carry):
        part = rows(block * BLOCK, BLOCK)
        queries, vals = q[part, :], v[part, :]
        scores = lax.dot_general(
            queries, k[part, :], (((1,), (1,)), ((), ())), preferred_element_type=F32
        )
        weights = (scores * within[...]).astype(BF16)
        local = jnp.dot(weights, vals, preferred_element_type=F32)
        inter = jnp.dot(
            jnp.concatenate([queries, queries], axis=1),
            jnp.concatenate(split(before[block]), axis=0),
            preferred_element_type=F32,
        )
        raw[part, :] = local + lead[...] * inter
        return carry

    read_q.wait()
    groups = 4
    group_blocks = blocks // groups

    duty = jnp.where(is_far, TURN, groups)

    @pl.loop(0, groups + 1)
    def _(group):
        @pl.when(jnp.logical_and(is_hub, group == duty))
        def _():
            gathered[me] = own[my_spot]
            state = jnp.zeros(gathered.shape[1:], F32)
            for step in range(n_seq):
                if step % quarter == 0:
                    group_sem = recv_sems.at[step // quarter]

                    @pl.when(me // quarter != step // quarter)
                    def _():
                        drain(group_sem, gathered, quarter)

                    if quarter > 1:
                        @pl.when(me // quarter == step // quarter)
                        def _():
                            drain(group_sem, gathered, quarter - 1)

                prefix[step] = state
                state = state * whole + gathered[step]
            lower, upper = state[:share, :], state[share:2 * share, :]
            last[0] = jnp.where(core == 1, upper, lower)
            last[1] = jnp.where(core == 1, lower, upper)
            last[2] = state[3 * share:, :]
            last[3] = state[2 * share:3 * share, :]

            @pl.loop(0, jnp.minimum(mine, far))
            def _(head):
                @pl.when(jnp.logical_not(jnp.logical_and(skip, head == 0)))
                def _():
                    ending(0, head).start()

                for which in (1, 2, 3):
                    ending(which, head).start()

            landed[my_spot] = prefix[me]

            for start in (n_seq // 2, 0):
                @pl.loop(0, n_seq // 2)
                def _(step):
                    to = start + lax.rem(me + step, n_seq // 2)

                    @pl.when(to != me)
                    def _():
                        entering(to).start()

            finals[mine] = last[0]
            for which in (1, 2, 3):
                ending(which, mine).start()

            @pl.loop(far, mine)
            def _(head):
                for which in range(4):
                    ending(which, head).start()

            @pl.when(mine < n_head - 1)
            def _():
                pl.semaphore_wait(ready, 4 * (n_head - 1 - mine))

            @pl.loop(mine + 1, n_head)
            def _(head):
                for which in range(4):
                    ending(which, head).start()

        @pl.when(group < groups)
        def _():
            for j in range(group_blocks):
                attend(group * group_blocks + j, 0)

    read_gain.wait()

    @pl.when(is_hub)
    def _():
        if n_hubs > 1:
            drain(recv_sems.at[4], landed, n_hubs - 1)

    @pl.when(jnp.logical_not(is_hub))
    def _():
        drain(recv_sems.at[4], landed, n_hubs)

    parts = [None] * (2 * n_hubs)
    for spot in range(n_hubs):
        for slot, seat in enumerate(seats[spot]):
            parts[seat] = landed[spot, 2 * share * slot:2 * share * (slot + 1), :]
    prior = jnp.concatenate(split(jnp.concatenate(parts, axis=0)), axis=0)

    def finish(piece, ahead):
        for j in range(blocks // 2):
            part = rows((piece * (blocks // 2) + j) * BLOCK, BLOCK)
            queries = q[part, :]
            inter = jnp.dot(
                jnp.concatenate([queries, queries], axis=1), prior, preferred_element_type=F32
            )
            value = raw[part, :] + (lead[...] * ahead) * inter
            mean_sq = jnp.mean(value * value, axis=-1, keepdims=True)
            out[part, :] = (value * lax.rsqrt(mean_sq + 1e-06) * gain[...]).astype(BF16)
            ahead = ahead * decay
        return ahead

    lax.fori_loop(0, 2, finish, ones)

    @pl.when(is_hub)
    def _():
        if n_hubs > 1:
            drain(send_sems.at[0], own, n_hubs - 1)
        drain(send_sems.at[1], prefix, n_seq - 1)
        for _ in range(3):
            drain(send_sems.at[2], finals, n_head)

        @pl.when(skip)
        def _():
            if n_head > 2:
                drain(send_sems.at[2], finals, n_head - 2)

        @pl.when(jnp.logical_not(skip))
        def _():
            drain(send_sems.at[2], finals, n_head - 1)

    @pl.when(jnp.logical_not(is_hub))
    def _():
        drain(send_sems.at[0], own, n_hubs)

    @pl.when(is_far)
    def _():
        to_early.wait_send()

    @pl.when(is_early)
    def _():
        drain(recv_sems.at[5], finals, far)
        pltpu.make_async_copy(direct, direct, recv_sems.at[6]).wait()
        for head in range(far, n_head):
            finals[head] = jnp.sum(direct[head - far], axis=0)

    @pl.when(jnp.logical_and(is_hub, jnp.logical_not(is_early)))
    def _():
        drain(recv_sems.at[5], finals, n_head - 1)

    @pl.when(jnp.logical_not(jnp.logical_or(is_hub, is_early)))
    def _():
        drain(recv_sems.at[5], finals, n_head)

    final[...] = finals[...]


def write_kernel(out, final, out_hbm, final_hbm, sems):
    piece_rows = out.shape[0] // PIECES
    copies = [pltpu.make_async_copy(final, final_hbm, sems.at[PIECES])]
    for piece in range(PIECES):
        part = pl.ds(piece * piece_rows, piece_rows)
        copies.append(pltpu.make_async_copy(out.at[part], out_hbm.at[part], sems.at[piece]))
    for copy in copies:
        copy.start()
    for copy in copies:
        copy.wait()


def on_device(n_seq, n_head, queries, keys, values, exponents, gain):
    tokens, width = queries.shape
    share = width // n_seq
    n_hubs = n_seq // 4
    vmem = pl.BlockSpec(memory_space=pltpu.VMEM)
    anywhere = pl.BlockSpec(memory_space=pl.ANY)
    hbm = pl.BlockSpec(memory_space=pltpu.HBM)
    blocks = tokens // BLOCK
    kept = pl.pallas_call(
        functools.partial(state_kernel, n_seq, n_head),
        out_shape=(
            pltpu.VMEM((tokens, width), BF16),
            pltpu.VMEM((n_head, share, width), F32),
        ),
        in_specs=[anywhere] + [hbm] * 4,
        out_specs=(vmem,) * 2,
        scratch_shapes=[
            pltpu.VMEM((tokens, width), BF16),
            pltpu.VMEM((tokens, width), BF16),
            pltpu.VMEM((tokens, width), BF16),
            pltpu.VMEM((tokens, width), F32),
            pltpu.SMEM((1,), jnp.int32),
            pltpu.VMEM((1, width), F32),
            pltpu.VMEM((BLOCK, BLOCK), F32),
            pltpu.VMEM((BLOCK, width), F32),
            pltpu.VMEM((BLOCK, width), F32),
            pltpu.VMEM((blocks, width, width), F32),
            pltpu.VMEM((n_hubs, 4 * share, width), F32),
            pltpu.VMEM((n_seq, 4 * share, width), F32),
            pltpu.VMEM((n_seq, 4 * share, width), F32),
            pltpu.VMEM((n_hubs, 4 * share, width), F32),
            pltpu.VMEM((4, share, width), F32),
            pltpu.VMEM((n_head, share, width), F32),
            pltpu.VMEM((share, width), F32),
            pltpu.VMEM((n_head - n_head // 2, n_seq, share, width), F32),
            pltpu.SemaphoreType.DMA((3, PIECES)),
            pltpu.SemaphoreType.DMA((2,)),
            pltpu.SemaphoreType.DMA((4,)),
            pltpu.SemaphoreType.DMA((7,)),
            pltpu.SemaphoreType.REGULAR,
        ],
        compiler_params=pltpu.CompilerParams(
            collective_id=0, has_side_effects=True, vmem_limit_bytes=40 * 1024 * 1024
        ),
        name="state",
    )(exponents, *(
        pltpu.with_memory_space_constraint(array, pltpu.HBM)
        for array in (gain.reshape(1, width), queries, keys, values)
    ))
    return pl.pallas_call(
        write_kernel,
        out_shape=(
            jax.ShapeDtypeStruct((tokens, width), BF16),
            jax.ShapeDtypeStruct((n_head, share, width), F32),
        ),
        in_specs=[vmem] * 2,
        out_specs=(anywhere, anywhere),
        scratch_shapes=[pltpu.SemaphoreType.DMA((PIECES + 1,))],
        compiler_params=pltpu.CompilerParams(vmem_limit_bytes=32 * 1024 * 1024),
        name="write",
    )(*kept)


def solution(mesh):
    return jax.shard_map(
        functools.partial(on_device, mesh.shape["seq"], mesh.shape["head"]),
        mesh=mesh,
        in_specs=(P("seq", "head"), P("seq", "head"), P("seq", "head"), P("head"), P("head")),
        out_specs=(P("seq", "head"), P(None, "seq", None)),
        check_vma=False,
    )
```

```python
import functools

import jax
import jax.numpy as jnp
from jax import lax
from jax.experimental import pallas as pl
from jax.experimental.pallas import tpu as pltpu
from jax.sharding import PartitionSpec as P

BLOCK = 256
PIECES = 2
EARLY = 1
URGENT = (0, 1, 4, 6)
TURN = 2
MESH = pl.DeviceIdType.MESH
F32 = jnp.float32
BF16 = jnp.bfloat16


def hub_chips(chips):
    if chips == 16:
        return ((0, 7), (1, 6), (2, 14), (3, 11), (4, 9), (5, 10), (8, 13), (12, 15))
    return tuple((chip, chips - 1 - chip) for chip in range(chips // 2))


def pick(index, table):
    value = jnp.int32(table[0])
    for entry in range(1, len(table)):
        value = jnp.where(index == entry, jnp.int32(table[entry]), value)
    return value


def rows(start, count):
    return pl.ds(pl.multiple_of(start, count), count)


def split(value):
    high = value.astype(BF16)
    return high, (value - high.astype(F32)).astype(BF16)


def state_kernel(
    n_seq, n_head,
    exps_hbm, gain_hbm, q_hbm, k_hbm, v_hbm,
    out, final,
    q, k, v, raw, exps, gain, within, lead, tail, before, own, gathered, prefix, landed,
    last, finals, toward, direct, in_sems, small_sems, send_sems, recv_sems, ready,
):
    me, mine = lax.axis_index("seq"), lax.axis_index("head")
    n_hubs = n_seq // 4
    tokens, width = q.shape
    blocks = tokens // BLOCK
    per_piece = blocks // PIECES
    share = width // n_seq
    def load(which, piece):
        src, dst = ((k_hbm, k), (v_hbm, v))[which]
        part = rows(piece * per_piece * BLOCK, per_piece * BLOCK)
        return pltpu.make_async_copy(src.at[part], dst.at[part], in_sems.at[which, piece])

    read_exps = pltpu.make_async_copy(exps_hbm, exps, small_sems.at[0])
    read_q = pltpu.make_async_copy(q_hbm, q, in_sems.at[2, 0])
    read_gain = pltpu.make_async_copy(gain_hbm, gain, small_sems.at[1])
    read_exps.start()
    for piece in range(PIECES):
        load(0, piece).start()
        load(1, piece).start()
    read_gain.start()

    seats = hub_chips(2 * n_hubs)
    seat_spots = {chip: spot for spot, pair in enumerate(seats) for chip in pair}
    my_spot = pick(me // 2, [seat_spots[chip] for chip in range(2 * n_hubs)])
    other = pick(my_spot, [pair[1] for pair in seats])
    home = 2 * pick(my_spot, [pair[0] for pair in seats]) + 1
    core = lax.rem(me, 2)
    targets = (me, 2 * (me // 2) + 1 - core, 2 * other + 1, 2 * other)

    def hub(first, head):
        return first - jnp.logical_and(first == EARLY, head == 0).astype(jnp.int32)

    is_hub = hub(home, mine) == me
    hub_count = is_hub.astype(jnp.int32)
    far = n_head // 2
    is_far = mine >= far
    skip = jnp.logical_and(me == EARLY, is_far)
    is_early = jnp.logical_and(me == EARLY, mine == 0)
    quarter = n_seq // 4

    barrier = pltpu.get_barrier_semaphore()

    def signal(sem, seq, head):
        pl.semaphore_signal(
            sem, inc=1, device_id={"seq": seq, "head": head}, device_id_type=MESH
        )

    @pl.when(is_hub)
    def _():
        @pl.loop(0, n_seq)
        def _(step):
            to = n_seq - 1 - step

            @pl.when(to != me)
            def _():
                signal(barrier, to, mine)

        @pl.loop(mine + 1, n_head)
        def _(head):
            for target in targets:
                signal(barrier, target, head)

    @pl.loop(mine + 1, n_head)
    def _(head):
        signal(barrier, hub(home, head), head)

    @pl.when(is_early)
    def _():
        @pl.loop(far, n_head)
        def _(head):
            @pl.loop(0, n_seq)
            def _(seq):
                signal(barrier, seq, head)

    read_exps.wait()
    rate = exps[0].astype(F32) / 16777216.0
    row = lax.broadcasted_iota(jnp.int32, (BLOCK, width), 0).astype(F32)
    tail[...] = jnp.exp2(-rate * (BLOCK - 1.0 - row))
    ones = jnp.ones((1, width), F32)
    decay = jnp.exp2(-rate * BLOCK * ones)
    whole = jnp.exp2(-rate * tokens * ones)

    def add(piece, total):
        load(0, piece).wait()
        load(1, piece).wait()
        for j in range(per_piece):
            block = piece * per_piece + j
            part = rows(block * BLOCK, BLOCK)
            scaled = (k[part, :].astype(F32) * tail[...]).astype(BF16)
            term = lax.dot_general(
                scaled, v[part, :], (((0,), (0,)), ((), ())), preferred_element_type=F32
            )
            before[block] = total
            total = total * decay + term
        return total

    total = lax.fori_loop(0, PIECES, add, jnp.zeros((width, width), F32))
    read_q.start()
    for spot in range(n_hubs):
        for slot, seat in enumerate(seats[spot]):
            own[spot, 2 * share * slot:2 * share * (slot + 1), :] = (
                total[2 * share * seat:2 * share * (seat + 1), :]
            )
    left = (n_seq - 1 - me).astype(F32) * tokens
    toward[...] = total[EARLY * share:(EARLY + 1) * share, :] * jnp.exp2(-rate * left * ones)

    pl.semaphore_wait(
        barrier, n_hubs - hub_count + mine * (1 + 4 * hub_count) + is_far.astype(jnp.int32)
    )

    def contribution(to, spot):
        return pltpu.make_async_remote_copy(
            src_ref=own.at[spot], dst_ref=gathered.at[me], send_sem=send_sems.at[0],
            recv_sem=recv_sems.at[me // quarter], device_id={"seq": to, "head": mine}, device_id_type=MESH,
        )

    def entering(to):
        return pltpu.make_async_remote_copy(
            src_ref=prefix.at[to], dst_ref=landed.at[my_spot], send_sem=send_sems.at[1],
            recv_sem=recv_sems.at[4], device_id={"seq": to, "head": mine}, device_id_type=MESH,
        )

    def ending(which, head):
        return pltpu.make_async_remote_copy(
            src_ref=last.at[which], dst_ref=finals.at[mine], send_sem=send_sems.at[2],
            recv_sem=recv_sems.at[5], device_id={"seq": targets[which], "head": head},
            device_id_type=MESH,
        )

    to_early = pltpu.make_async_remote_copy(
        src_ref=toward, dst_ref=direct.at[jnp.maximum(mine - far, 0), me], send_sem=send_sems.at[3],
        recv_sem=recv_sems.at[6], device_id={"seq": EARLY, "head": 0}, device_id_type=MESH,
    )

    @pl.when(is_far)
    def _():
        to_early.start()

    def drain(sem, ref, count):
        part = ref.at[pl.ds(0, count)]
        pltpu.make_async_copy(part, part, sem).wait()

    def contribute(order):
        for spot in order:
            to = hub(jnp.int32(2 * seats[spot][0] + 1), mine)

            @pl.when(me != to)
            def _():
                contribution(to, spot).start()

    contribute(sorted(range(n_hubs), key=lambda spot: URGENT.index(spot) if spot in URGENT else n_hubs))

    @pl.loop(0, mine)
    def _(head):
        signal(ready, hub(home, head), head)

    lead[...] = jnp.exp2(-rate * (row + 1.0))
    gap = (
        lax.broadcasted_iota(jnp.int32, (BLOCK, BLOCK), 0)
        - lax.broadcasted_iota(jnp.int32, (BLOCK, BLOCK), 1)
    ).astype(F32)
    within[...] = jnp.where(gap >= 0.0, jnp.exp2(-rate * jnp.maximum(gap, 0.0)), 0.0)

    def attend(block, carry):
        part = rows(block * BLOCK, BLOCK)
        queries, vals = q[part, :], v[part, :]
        scores = lax.dot_general(
            queries, k[part, :], (((1,), (1,)), ((), ())), preferred_element_type=F32
        )
        weights = (scores * within[...]).astype(BF16)
        local = jnp.dot(weights, vals, preferred_element_type=F32)
        inter = jnp.dot(
            jnp.concatenate([queries, queries], axis=1),
            jnp.concatenate(split(before[block]), axis=0),
            preferred_element_type=F32,
        )
        raw[part, :] = local + lead[...] * inter
        return carry

    read_q.wait()
    groups = 4
    group_blocks = blocks // groups

    duty = jnp.where(is_far, TURN, groups)

    @pl.loop(0, groups + 1)
    def _(group):
        @pl.when(jnp.logical_and(is_hub, group == duty))
        def _():
            gathered[me] = own[my_spot]
            state = jnp.zeros(gathered.shape[1:], F32)
            for step in range(n_seq):
                if step % quarter == 0:
                    group_sem = recv_sems.at[step // quarter]

                    @pl.when(me // quarter != step // quarter)
                    def _():
                        drain(group_sem, gathered, quarter)

                    if quarter > 1:
                        @pl.when(me // quarter == step // quarter)
                        def _():
                            drain(group_sem, gathered, quarter - 1)

                prefix[step] = state
                state = state * whole + gathered[step]
            lower, upper = state[:share, :], state[share:2 * share, :]
            last[0] = jnp.where(core == 1, upper, lower)
            last[1] = jnp.where(core == 1, lower, upper)
            last[2] = state[3 * share:, :]
            last[3] = state[2 * share:3 * share, :]

            @pl.loop(0, jnp.minimum(mine, far))
            def _(head):
                @pl.when(jnp.logical_not(jnp.logical_and(skip, head == 0)))
                def _():
                    ending(0, head).start()

                for which in (1, 2, 3):
                    ending(which, head).start()

            landed[my_spot] = prefix[me]

            for start in (n_seq // 2, 0):
                @pl.loop(0, n_seq // 2)
                def _(step):
                    to = start + lax.rem(me + step, n_seq // 2)

                    @pl.when(to != me)
                    def _():
                        entering(to).start()

            finals[mine] = last[0]
            for which in (1, 2, 3):
                ending(which, mine).start()

            @pl.loop(far, mine)
            def _(head):
                for which in range(4):
                    ending(which, head).start()

            @pl.when(mine < n_head - 1)
            def _():
                pl.semaphore_wait(ready, 4 * (n_head - 1 - mine))

            @pl.loop(mine + 1, n_head)
            def _(head):
                for which in range(4):
                    ending(which, head).start()

        @pl.when(group < groups)
        def _():
            for j in range(group_blocks):
                attend(group * group_blocks + j, 0)

    read_gain.wait()

    @pl.when(is_hub)
    def _():
        if n_hubs > 1:
            drain(recv_sems.at[4], landed, n_hubs - 1)

    @pl.when(jnp.logical_not(is_hub))
    def _():
        drain(recv_sems.at[4], landed, n_hubs)

    parts = [None] * (2 * n_hubs)
    for spot in range(n_hubs):
        for slot, seat in enumerate(seats[spot]):
            parts[seat] = landed[spot, 2 * share * slot:2 * share * (slot + 1), :]
    prior = jnp.concatenate(split(jnp.concatenate(parts, axis=0)), axis=0)

    def finish(piece, ahead):
        for j in range(blocks // 2):
            part = rows((piece * (blocks // 2) + j) * BLOCK, BLOCK)
            queries = q[part, :]
            inter = jnp.dot(
                jnp.concatenate([queries, queries], axis=1), prior, preferred_element_type=F32
            )
            value = raw[part, :] + (lead[...] * ahead) * inter
            mean_sq = jnp.mean(value * value, axis=-1, keepdims=True)
            out[part, :] = (value * lax.rsqrt(mean_sq + 1e-06) * gain[...]).astype(BF16)
            ahead = ahead * decay
        return ahead

    lax.fori_loop(0, 2, finish, ones)

    @pl.when(is_hub)
    def _():
        if n_hubs > 1:
            drain(send_sems.at[0], own, n_hubs - 1)
        drain(send_sems.at[1], prefix, n_seq - 1)
        for _ in range(3):
            drain(send_sems.at[2], finals, n_head)

        @pl.when(skip)
        def _():
            if n_head > 2:
                drain(send_sems.at[2], finals, n_head - 2)

        @pl.when(jnp.logical_not(skip))
        def _():
            drain(send_sems.at[2], finals, n_head - 1)

    @pl.when(jnp.logical_not(is_hub))
    def _():
        drain(send_sems.at[0], own, n_hubs)

    @pl.when(is_far)
    def _():
        to_early.wait_send()

    @pl.when(is_early)
    def _():
        drain(recv_sems.at[5], finals, far)
        pltpu.make_async_copy(direct, direct, recv_sems.at[6]).wait()
        for head in range(far, n_head):
            finals[head] = jnp.sum(direct[head - far], axis=0)

    @pl.when(jnp.logical_and(is_hub, jnp.logical_not(is_early)))
    def _():
        drain(recv_sems.at[5], finals, n_head - 1)

    @pl.when(jnp.logical_not(jnp.logical_or(is_hub, is_early)))
    def _():
        drain(recv_sems.at[5], finals, n_head)

    final[...] = finals[...]


def write_kernel(out, final, out_hbm, final_hbm, sems):
    piece_rows = out.shape[0] // 4
    copies = [pltpu.make_async_copy(final, final_hbm, sems.at[4])]
    for piece in range(4):
        part = pl.ds(piece * piece_rows, piece_rows)
        copies.append(pltpu.make_async_copy(out.at[part], out_hbm.at[part], sems.at[piece]))
    for copy in copies:
        copy.start()
    for copy in copies:
        copy.wait()


def on_device(n_seq, n_head, queries, keys, values, exponents, gain):
    tokens, width = queries.shape
    share = width // n_seq
    n_hubs = n_seq // 4
    vmem = pl.BlockSpec(memory_space=pltpu.VMEM)
    anywhere = pl.BlockSpec(memory_space=pl.ANY)
    hbm = pl.BlockSpec(memory_space=pltpu.HBM)
    blocks = tokens // BLOCK
    kept = pl.pallas_call(
        functools.partial(state_kernel, n_seq, n_head),
        out_shape=(
            pltpu.VMEM((tokens, width), BF16),
            pltpu.VMEM((n_head, share, width), F32),
        ),
        in_specs=[anywhere] + [hbm] * 4,
        out_specs=(vmem,) * 2,
        scratch_shapes=[
            pltpu.VMEM((tokens, width), BF16),
            pltpu.VMEM((tokens, width), BF16),
            pltpu.VMEM((tokens, width), BF16),
            pltpu.VMEM((tokens, width), F32),
            pltpu.SMEM((1,), jnp.int32),
            pltpu.VMEM((1, width), F32),
            pltpu.VMEM((BLOCK, BLOCK), F32),
            pltpu.VMEM((BLOCK, width), F32),
            pltpu.VMEM((BLOCK, width), F32),
            pltpu.VMEM((blocks, width, width), F32),
            pltpu.VMEM((n_hubs, 4 * share, width), F32),
            pltpu.VMEM((n_seq, 4 * share, width), F32),
            pltpu.VMEM((n_seq, 4 * share, width), F32),
            pltpu.VMEM((n_hubs, 4 * share, width), F32),
            pltpu.VMEM((4, share, width), F32),
            pltpu.VMEM((n_head, share, width), F32),
            pltpu.VMEM((share, width), F32),
            pltpu.VMEM((n_head - n_head // 2, n_seq, share, width), F32),
            pltpu.SemaphoreType.DMA((3, PIECES)),
            pltpu.SemaphoreType.DMA((2,)),
            pltpu.SemaphoreType.DMA((4,)),
            pltpu.SemaphoreType.DMA((7,)),
            pltpu.SemaphoreType.REGULAR,
        ],
        compiler_params=pltpu.CompilerParams(
            collective_id=0, has_side_effects=True, vmem_limit_bytes=40 * 1024 * 1024
        ),
        name="state",
    )(exponents, *(
        pltpu.with_memory_space_constraint(array, pltpu.HBM)
        for array in (gain.reshape(1, width), queries, keys, values)
    ))
    return pl.pallas_call(
        write_kernel,
        out_shape=(
            jax.ShapeDtypeStruct((tokens, width), BF16),
            jax.ShapeDtypeStruct((n_head, share, width), F32),
        ),
        in_specs=[vmem] * 2,
        out_specs=(anywhere, anywhere),
        scratch_shapes=[pltpu.SemaphoreType.DMA((5,))],
        compiler_params=pltpu.CompilerParams(vmem_limit_bytes=32 * 1024 * 1024),
        name="write",
    )(*kept)


def solution(mesh):
    return jax.shard_map(
        functools.partial(on_device, mesh.shape["seq"], mesh.shape["head"]),
        mesh=mesh,
        in_specs=(P("seq", "head"), P("seq", "head"), P("seq", "head"), P("head"), P("head")),
        out_specs=(P("seq", "head"), P(None, "seq", None)),
        check_vma=False,
    )
```
